512 devices in a mesh: blk: 16 (over x_lo, z), wide: 32 (over y, x_hi, core).
Axes of the slice: x: 4 (x_hi: 2, x_lo: 2; x = x_hi * 2 + x_lo), y: 8, z: 8, core: 2. Of those that a mesh axis runs over, the one named last changes fastest.
Arguments:
- q_latent: bfloat16 [4096, 1536], P(('blk', 'wide')), may hold values from -768 to 768
- kv_raw: bfloat16 [4096, 576], P(('blk', 'wide')), may hold values from -600 to 600
- query_plain_weight: bfloat16 [1536, 8192], P('blk', 'wide'), may hold values from -0.15625 to 0.15625
- query_rotary_weight: bfloat16 [1536, 4096], P('blk', 'wide'), may hold values from -0.15625 to 0.15625
- key_up_weight: bfloat16 [512, 8192], P('blk', 'wide'), may hold values from -0.25 to 0.25
- value_up_weight: bfloat16 [512, 8192], P('blk', 'wide'), may hold values from -0.59765625 to 0.59765625
- doc_starts: int32 [24], replicated, may hold values from 0 to 4095, as said below
- tile_kind: int32 [32, 32], P('blk'), may hold values from 0 to 2, as said below
Outputs:
- attended: bfloat16 [4096, 8192], P('blk', 'wide')
The draws below stay inside these ranges and needn't reach their ends.
Inputs may be any that keep to these rules, and one draw needn't show every extreme that they name: doc_starts[0] = 0 and the starts rise strictly; a document runs to the next start, the last one to 4096; the longest has exactly 3072 tokens. tile_kind[i, j] is 1 where every token pair of query tile i and key tile j lies in one document with the key not after the query, 0 where no pair does, 2 otherwise; diagonal tiles are 2, so a token always sees itself.
All inputs are finite; a program needn't handle non-finite values.
Results may differ from the reference program's by a relative error of at most 0.012.
The reference program's roundings to bfloat16 on the way (of `kv_normed`, `q_nope`, `query`, `weights` and `latent_out`) count: a program that leaves them out, or rounds other values in their place, can miss the bound.
Values may be sent and summed in bfloat16 or wider, within the bound.
No kernel may reach another device: no remote copies, remote signals or barrier semaphores. Data moves between devices by JAX's collectives and lax.ppermute only.
A program may use at most 64 MiB of HBM per device.

```python
import math
import jax
import jax.numpy as jnp
from jax import lax

QUERY_LATENT = 1536
LATENT_WIDTH = 512
ROTARY_DIMS = 64
PLAIN_QUERY_DIMS = 128
VALUE_DIMS = 128
TILE = 128
DOCS = 24
TOK_DEV = 256
ATTENTION_HEADS = 64
PACKED_TOKENS = 4096
MOST = 3072
TILES = 32
N_BLK = 16


def doc_lengths(key):
    remainder = PACKED_TOKENS - MOST
    cut_key = jax.random.fold_in(key, 101)
    place_key = jax.random.fold_in(key, 102)
    candidates = jax.random.permutation(cut_key, remainder - 1) + 1
    cut_points = jnp.sort(candidates[:DOCS - 2]).astype(jnp.int32)
    boundary = jnp.concatenate([jnp.zeros((1,), jnp.int32), cut_points, jnp.full((1,), remainder, jnp.int32)])
    pieces = boundary[1:] - boundary[:-1]
    long_slot = jax.random.randint(place_key, (), 0, DOCS)
    places = jnp.arange(DOCS, dtype=jnp.int32)
    earlier_piece = pieces[jnp.clip(places, 0, DOCS - 2)]
    later_piece = pieces[jnp.clip(places - 1, 0, DOCS - 2)]
    lengths = jnp.where(places < long_slot, earlier_piece, later_piece)
    return jnp.where(places == long_slot, MOST, lengths).astype(jnp.int32)


def doc_start_list(key):
    lengths = doc_lengths(key)
    return (jnp.cumsum(lengths) - lengths).astype(jnp.int32)


def draw_doc_starts(key, part):
    starts = doc_start_list(key)
    return starts


def draw_tile_kind(key, part):
    starts = doc_start_list(key)
    positions = jnp.arange(PACKED_TOKENS, dtype=jnp.int32)
    owner = jnp.sum((starts[None, :] <= positions[:, None]).astype(jnp.int32), axis=1) - 1
    heads_doc = owner[::TILE]
    tails_doc = owner[TILE - 1::TILE]
    row_tiles = jnp.arange(TILES, dtype=jnp.int32)[:, None]
    col_tiles = jnp.arange(TILES, dtype=jnp.int32)[None, :]
    touching = tails_doc[None, :] == heads_doc[:, None]
    covering = heads_doc[None, :] == tails_doc[:, None]
    earlier = jnp.where(touching, jnp.where(covering, 1, 2), 0)
    kinds = jnp.where(col_tiles < row_tiles, earlier, jnp.where(col_tiles == row_tiles, 2, 0))
    return kinds.astype(jnp.int32)


def draw_q_latent(key, part):
    key = jax.random.fold_in(key, 7)
    random_seed_key = jax.random.fold_in(key, 0)
    value_matrix = jnp.clip(jax.random.normal(random_seed_key, (PACKED_TOKENS, QUERY_LATENT), jnp.float32), -6.0, 6.0)
    return value_matrix.astype(jnp.bfloat16)


def draw_kv_raw(key, part):
    key = jax.random.fold_in(key, 9)
    random_seed_key, row_key, col_key = jax.random.split(key, 3)
    combined_width = LATENT_WIDTH + ROTARY_DIMS
    value_matrix = jnp.clip(jax.random.normal(random_seed_key, (PACKED_TOKENS, combined_width), jnp.float32), -6.0, 6.0)
    row_scale = jnp.exp(jax.random.uniform(row_key, (PACKED_TOKENS, 1), jnp.float32) * math.log(10.0))
    col_scale = jnp.exp(jax.random.uniform(col_key, (1, combined_width), jnp.float32) * math.log(10.0))
    latent_columns = jnp.arange(combined_width)[None, :] < LATENT_WIDTH
    value_matrix = value_matrix * jnp.where(latent_columns, row_scale * col_scale, 1.0)
    return value_matrix.astype(jnp.bfloat16)


def block_scale(stream_key, extent, cuts, smallest, top_value):
    def one(position, blocks):
        steps = jax.random.uniform(jax.random.fold_in(jax.random.fold_in(stream_key, 6), position), (blocks,), jnp.float32, smallest / len(cuts), top_value / len(cuts))
        return jnp.repeat(jnp.exp(steps), extent[position] // blocks).reshape((-1,) + (1,) * (len(extent) - position - 1))

    gain = one(*cuts[0])
    for cut in cuts[1:]:
        gain = gain * one(*cut)
    return gain


def noise(rng, shape, width, bound, cuts=(), kind=jnp.bfloat16):
    values = width * jax.random.normal(rng, shape, jnp.float32)
    if cuts:
        values = values * block_scale(rng, shape, cuts, -0.22, 0.18)
    return jnp.clip(values, -bound, bound).astype(kind)


def setup_inputs(seed: int = 0) -> dict:
    streams_of = jax.random.split(jax.random.key(seed), 9)
    q_latent = draw_q_latent(jax.random.fold_in(streams_of[8], 71), 0)
    kv_raw = draw_kv_raw(jax.random.fold_in(streams_of[8], 71), 0)
    query_plain_weight = noise(streams_of[2], (QUERY_LATENT, ATTENTION_HEADS * PLAIN_QUERY_DIMS), QUERY_LATENT ** -0.5, 0.15625, ((0, 16), (1, 32)))
    query_rotary_weight = noise(streams_of[3], (QUERY_LATENT, ATTENTION_HEADS * ROTARY_DIMS), QUERY_LATENT ** -0.5, 0.15625, ((0, 16), (1, 32)))
    key_up_weight = noise(streams_of[4], (LATENT_WIDTH, ATTENTION_HEADS * PLAIN_QUERY_DIMS), LATENT_WIDTH ** -0.5, 0.25, ((0, 16), (1, 32)))
    value_up_weight = noise(streams_of[5], (LATENT_WIDTH, ATTENTION_HEADS * VALUE_DIMS), 0.1, 0.59765625, ((0, 16), (1, 32)))
    doc_starts = draw_doc_starts(jax.random.fold_in(streams_of[8], 71), 0)
    tile_kind = draw_tile_kind(jax.random.fold_in(streams_of[8], 71), 0)
    return {"q_latent": q_latent, "kv_raw": kv_raw, "query_plain_weight": query_plain_weight, "query_rotary_weight": query_rotary_weight, "key_up_weight": key_up_weight, "value_up_weight": value_up_weight, "doc_starts": doc_starts, "tile_kind": tile_kind}


def normalize_latent(kv_raw):
    value_matrix = kv_raw.astype(jnp.float32)
    latent_vectors = value_matrix[:, :LATENT_WIDTH]
    energy = lax.optimization_barrier(jnp.mean(latent_vectors * latent_vectors, axis=1, keepdims=True))
    scaled_scores = latent_vectors * lax.rsqrt(energy + 1e-06)
    return jnp.concatenate([scaled_scores, value_matrix[:, LATENT_WIDTH:]], axis=1).astype(jnp.bfloat16)

def document_of(positions, doc_starts):
    return lax.optimization_barrier(jnp.sum((doc_starts[None, :] <= positions[:, None]).astype(jnp.int32), axis=1)) - 1

def rounded(value_matrix):
    return lax.optimization_barrier(value_matrix.astype(jnp.bfloat16)).astype(jnp.float32)

def reference(q_latent, kv_raw, query_plain_weight, query_rotary_weight, key_up_weight, value_up_weight, doc_starts, tile_kind):
    kv_normed = lax.optimization_barrier(normalize_latent(kv_raw))
    q_nope = rounded(jnp.dot(q_latent, query_plain_weight, preferred_element_type=jnp.float32)).reshape(PACKED_TOKENS, ATTENTION_HEADS, PLAIN_QUERY_DIMS)
    q_rope = jnp.dot(q_latent, query_rotary_weight, preferred_element_type=jnp.float32).astype(jnp.bfloat16)
    q_rope = q_rope.reshape(PACKED_TOKENS, ATTENTION_HEADS, ROTARY_DIMS)
    per_head_keys = key_up_weight.astype(jnp.float32).reshape(LATENT_WIDTH, ATTENTION_HEADS, PLAIN_QUERY_DIMS)
    q_absorbed = jnp.einsum('thn,chn->thc', q_nope, per_head_keys).astype(jnp.bfloat16)
    query = lax.optimization_barrier(jnp.concatenate([q_absorbed, q_rope], axis=2))
    positions = jnp.arange(PACKED_TOKENS, dtype=jnp.int32)
    doc_index = document_of(positions, doc_starts)
    key_matrix = kv_normed.astype(jnp.float32)
    value_portion = key_matrix[:, :LATENT_WIDTH]
    per_head_values = value_up_weight.astype(jnp.float32).reshape(LATENT_WIDTH, ATTENTION_HEADS, VALUE_DIMS)
    key_tiles = positions // TILE
    scale = (PLAIN_QUERY_DIMS + ROTARY_DIMS) ** (-0.5)

    def one_block(block):
        first = (block * TOK_DEV).astype(jnp.int32)
        rows = lax.dynamic_slice_in_dim(query, first, TOK_DEV, 0).astype(jnp.float32)
        q_pos = first + jnp.arange(TOK_DEV, dtype=jnp.int32)
        q_doc = lax.dynamic_slice_in_dim(doc_index, first, TOK_DEV, 0)
        kind_rows = tile_kind[q_pos // TILE][:, key_tiles]
        same_doc = q_doc[:, None] == doc_index[None, :]
        causal = positions[None, :] <= q_pos[:, None]
        allowed = (kind_rows == 1) | (kind_rows == 2) & same_doc & causal
        scores = jnp.einsum('thc,kc->thk', rows, key_matrix) * scale
        scores = jnp.where(allowed[:, None, :], scores, -jnp.inf)
        highest = lax.optimization_barrier(jnp.max(scores, axis=2))
        weights = jnp.exp(scores - highest[:, :, None])
        total = lax.optimization_barrier(jnp.sum(weights, axis=2))
        summed = jnp.einsum('thk,kc->thc', rounded(weights), value_portion)
        latent_out = rounded(summed / total[:, :, None])
        result = jnp.einsum('thc,chv->thv', latent_out, per_head_values).astype(jnp.bfloat16)
        return result.reshape(TOK_DEV, ATTENTION_HEADS * VALUE_DIMS)
    blocks = lax.map(one_block, jnp.arange(N_BLK, dtype=jnp.int32))
    return blocks.reshape(PACKED_TOKENS, ATTENTION_HEADS * VALUE_DIMS)
```

```python
import jax
import jax.numpy as jnp
import numpy as np
from jax import lax
from jax.experimental import pallas as pl
from jax.experimental.pallas import tpu as pltpu
from jax.sharding import Mesh, PartitionSpec as P

LATENT_WIDTH = 512
ROTARY_DIMS = 64
PLAIN_QUERY_DIMS = 128
VALUE_DIMS = 128
TILE = 128
WIDTH = 640
KEY_STEP = 512
SCALE = (PLAIN_QUERY_DIMS + ROTARY_DIMS) ** (-0.5)
LOG2E = 1.4426950408889634
NEG = -1e30

AXES = ("xl", "z", "y2", "y1", "xh", "c")
SIZES = (2, 8, 4, 2, 2, 2)
BLK = ("xl", "z")
WIDE = ("y2", "y1", "xh", "c")


def normalize_latent(kv_raw):
    value_matrix = kv_raw.astype(jnp.float32)
    latent_vectors = value_matrix[:, :LATENT_WIDTH]
    energy = jnp.mean(latent_vectors * latent_vectors, axis=1, keepdims=True)
    scaled = latent_vectors * lax.rsqrt(energy + 1e-06)
    return jnp.concatenate([scaled, value_matrix[:, LATENT_WIDTH:]], axis=1).astype(jnp.bfloat16)


def swap(x, axis):
    return lax.ppermute(x, axis, [(0, 1), (1, 0)])


def in_order(bit, own, other, axis):
    first = jnp.where(bit == 0, own, other)
    second = jnp.where(bit == 0, other, own)
    return jnp.concatenate([first, second], axis=axis)


def attention_kernel(q_ref, *refs):
    pieces = refs[:-6]
    low_ref, high_ref, bounds_ref, vu_ref, o_ref, s_ref = refs[-6:]
    q = q_ref[...]
    rows = q.shape[0]
    groups = rows // TILE
    half = groups // 2
    chunks = []
    at = 0
    for ref in pieces:
        for start in range(0, ref.shape[0], KEY_STEP):
            chunks.append((ref, start, at))
            at += KEY_STEP
    highest = [jnp.full((TILE, 128), NEG, jnp.float32) for _ in range(groups)]
    for ref, start, at in chunks:
        keys = ref[pl.ds(start, KEY_STEP), :]
        scores = lax.dot_general(
            q, keys, (((1,), (1,)), ((), ())), preferred_element_type=jnp.float32
        )
        for tile in range(half):
            last = bounds_ref[pl.ds(tile * TILE, TILE), 0:1]
            first = bounds_ref[pl.ds(tile * TILE, TILE), 1:2]
            low = low_ref[tile : tile + 1, pl.ds(at, KEY_STEP)]
            high = high_ref[tile : tile + 1, pl.ds(at, KEY_STEP)]
            allowed = (low <= last) & (high >= first)
            for head in range(2):
                g = head * half + tile
                part = jnp.where(allowed, scores[g * TILE : (g + 1) * TILE, :], NEG)
                s_ref[pl.ds(g * TILE, TILE), pl.ds(at, KEY_STEP)] = part
                top = highest[g]
                for lane in range(0, KEY_STEP, 128):
                    top = jnp.maximum(top, part[:, lane : lane + 128])
                highest[g] = top
    factor = SCALE * LOG2E
    peak = [jnp.max(h, axis=1, keepdims=True) for h in highest]
    sums = [jnp.zeros((TILE, 128), jnp.float32) for _ in range(groups)]
    accum = jnp.zeros((rows, LATENT_WIDTH), jnp.float32)
    for ref, start, at in chunks:
        parts = []
        for g in range(groups):
            part = s_ref[pl.ds(g * TILE, TILE), pl.ds(at, KEY_STEP)]
            weights = jnp.exp2((part - peak[g]) * factor)
            total = sums[g]
            for lane in range(0, KEY_STEP, 128):
                total = total + weights[:, lane : lane + 128]
            sums[g] = total
            parts.append(weights.astype(jnp.bfloat16))
        accum = accum + jnp.dot(
            jnp.concatenate(parts, axis=0),
            ref[pl.ds(start, KEY_STEP), 0:LATENT_WIDTH],
            preferred_element_type=jnp.float32,
        )
    totals = jnp.concatenate([jnp.sum(s, axis=1, keepdims=True) for s in sums], axis=0)
    latent_out = (accum / totals).astype(jnp.bfloat16)
    tokens = rows // 2
    for head in range(2):
        cols = pl.ds(head * VALUE_DIMS, VALUE_DIMS)
        o_ref[:, cols] = jnp.dot(
            latent_out[head * tokens : (head + 1) * tokens, :],
            vu_ref[:, cols],
            preferred_element_type=jnp.float32,
        ).astype(jnp.bfloat16)


def attention(query, pieces, low, high, bounds, value_up):
    tokens = query.shape[0] // 2
    count = low.shape[1]
    vmem = pl.BlockSpec(memory_space=pltpu.VMEM)
    return pl.pallas_call(
        attention_kernel,
        out_shape=jax.ShapeDtypeStruct((tokens, 2 * VALUE_DIMS), jnp.bfloat16),
        in_specs=[vmem] * (len(pieces) + 5),
        out_specs=vmem,
        scratch_shapes=[pltpu.VMEM((2 * tokens, count), jnp.float32)],
        compiler_params=pltpu.CompilerParams(vmem_limit_bytes=48 * 1024 * 1024),
        cost_estimate=pl.CostEstimate(
            flops=2 * 2 * tokens * count * (576 + 512),
            bytes_accessed=count * WIDTH * 2,
            transcendentals=2 * tokens * count,
        ),
    )(query, *pieces, low, high, bounds, value_up)


def body(
    q_latent,
    kv_raw,
    query_plain_weight,
    query_rotary_weight,
    key_up_weight,
    value_up_weight,
    doc_starts,
    tile_kind,
):
    xl, z = lax.axis_index("xl"), lax.axis_index("z")
    y1, xh, core = lax.axis_index("y1"), lax.axis_index("xh"), lax.axis_index("c")
    bf16 = jnp.bfloat16

    q_far = swap(q_latent, "xh")
    kv = normalize_latent(kv_raw)
    kv_rows = jnp.concatenate(
        [kv[:, 0:256], kv[:, 256:512], jnp.pad(kv[:, 512:576], ((0, 0), (0, 192))), jnp.zeros((8, 256), bf16)],
        axis=0,
    )
    right = jnp.concatenate([key_up_weight, value_up_weight, kv_rows], axis=0)
    packed = jnp.concatenate([query_plain_weight, query_rotary_weight, right], axis=1)
    by_z = lax.all_gather(packed, "z")
    w_other = swap(by_z, "xl")
    kv_z = jnp.concatenate(
        [by_z[:, 64:72, 384:640], by_z[:, 72:80, 384:640], by_z[:, 80:88, 384:512]], axis=2
    ).reshape(64, WIDTH)

    both = jnp.stack([q_latent, q_far], axis=0)
    q_rows = both.reshape(2, 8, 3, 512).transpose(2, 0, 1, 3).reshape(48, 512)
    q_rows = jnp.pad(q_rows, ((0, 0), (0, WIDTH - 512)))
    slot = jnp.concatenate([kv_z, q_rows], axis=0)
    by_y = lax.all_to_all(jnp.broadcast_to(slot[None], (4,) + slot.shape), "y2", 0, 0)
    near = by_y[:, 0:64, :].reshape(256, WIDTH)
    q_near = by_y[:, 64:112, 0:512]

    next_y = swap(near, "y1")
    x2_near = swap(near, "xh")
    q_next = swap(q_near, "y1")
    pair = jnp.concatenate([near, next_y], axis=0)
    x1_pair = swap(pair, "xl")
    x3_pair = lax.ppermute(pair, ("xl", "xh"), [(0, 3), (3, 0), (1, 2), (2, 1)])
    x2_next = swap(x2_near, "y1")
    x2_pair = jnp.concatenate([x2_near, x2_next], axis=0)

    def q_block(q_near, q_next):
        both_y = in_order(y1, q_near[:, None], q_next[:, None], 1)
        parts = both_y.reshape(4, 2, 3, 2, 8, 512)
        both_x = in_order(xh, parts[:, :, :, 0:1], parts[:, :, :, 1:2], 3)
        return both_x

    q_half = q_block(q_near, q_next)
    q_half = q_half.transpose(0, 1, 3, 4, 2, 5).reshape(16, 8, 1536)
    q_core = swap(q_half, "c")
    q_all = in_order(core, q_half[:, None], q_core[:, None], 1).reshape(256, 1536)

    def halves(x):
        return x[:, :, 0:384].reshape(768, 384)

    own_cols = jnp.where(xl == 0, q_all[:, 0:768], q_all[:, 768:1536])
    other_cols = jnp.where(xl == 0, q_all[:, 768:1536], q_all[:, 0:768])
    projected = jnp.dot(own_cols, halves(by_z), preferred_element_type=jnp.float32) + jnp.dot(
        other_cols, halves(w_other), preferred_element_type=jnp.float32
    )
    projected = projected.astype(bf16)

    def latent_rows(first):
        own = by_z[:, first : first + 32, 384:640].reshape(256, 256)
        other = w_other[:, first : first + 32, 384:640].reshape(256, 256)
        return in_order(xl, own, other, 0)

    key_up, value_up = latent_rows(0), latent_rows(32)
    heads = []
    for head in range(2):
        cols = slice(head * PLAIN_QUERY_DIMS, (head + 1) * PLAIN_QUERY_DIMS)
        absorbed = lax.dot_general(
            projected[:, cols], key_up[:, cols], (((1,), (1,)), ((), ())), preferred_element_type=jnp.float32
        ).astype(bf16)
        rope = projected[:, 256 + head * ROTARY_DIMS : 256 + (head + 1) * ROTARY_DIMS]
        heads.append(jnp.concatenate([absorbed, rope, jnp.zeros((256, 64), bf16)], axis=1))
    query = jnp.concatenate(heads, axis=0)

    mine = [pair, x1_pair, x2_pair, x3_pair]
    theirs = [swap(piece, "c") for piece in mine]

    shape = (2, 4, 2, 4, 8, 8)
    at = lambda d: lax.broadcasted_iota(jnp.int32, shape, d)
    far = at(1)
    k_xl, k_xh = xl ^ (far & 1), xh ^ (far >> 1)
    k_block = k_xl * 8 + at(4)
    k_y = 2 * at(3) + (y1 ^ at(2))
    k_pos = (k_block * 256 + ((k_y * 2 + k_xh) * 2 + (core ^ at(0))) * 8 + at(5)).reshape(1, 4096)
    k_tile = k_pos // TILE
    kinds = jnp.sum(
        jnp.where(
            lax.broadcasted_iota(jnp.int32, (1, 32, 4096), 1) == k_tile[:, None, :], tile_kind[:, :, None], 0
        ),
        axis=1,
    )
    big = jnp.int32(1 << 20)
    low = jnp.where(kinds == 2, k_pos, jnp.where(kinds == 1, -1, big))
    high = jnp.where(kinds == 2, k_pos, jnp.where(kinds == 1, big, -1))
    q_pos = (xl * 8 + z) * 256 + lax.broadcasted_iota(jnp.int32, (256, 1), 0)
    q_first = jnp.max(jnp.where(doc_starts[None, :] <= q_pos, doc_starts[None, :], 0), axis=1, keepdims=True)
    bounds = jnp.concatenate([q_pos, q_first], axis=1)
    return attention(query, mine + theirs, low, high, bounds, value_up)


def solution(mesh):
    fine = Mesh(np.asarray(mesh.devices).reshape(SIZES), AXES)
    return jax.shard_map(
        body,
        mesh=fine,
        in_specs=(
            P(AXES, None),
            P(AXES, None),
            P(BLK, WIDE),
            P(BLK, WIDE),
            P(BLK, WIDE),
            P(BLK, WIDE),
            P(),
            P(BLK, None),
        ),
        out_specs=P(BLK, WIDE),
        check_vma=False,
    )
```

```python
import jax
import jax.numpy as jnp
import numpy as np
from jax import lax
from jax.experimental import pallas as pl
from jax.experimental.pallas import tpu as pltpu
from jax.sharding import Mesh, PartitionSpec as P

LATENT_WIDTH = 512
ROTARY_DIMS = 64
PLAIN_QUERY_DIMS = 128
VALUE_DIMS = 128
TILE = 128
WIDTH = 640
KEY_STEP = 512
SCALE = (PLAIN_QUERY_DIMS + ROTARY_DIMS) ** (-0.5)
FACTOR = SCALE * 1.4426950408889634
NEG = -1e30
FLOOR = -1e29

AXES = ("xl", "z2", "z1", "y2", "y1", "xh", "c")
SIZES = (2, 4, 2, 4, 2, 2, 2)
Z = ("z2", "z1")
BLK = ("xl", "z2", "z1")
WIDE = ("y2", "y1", "xh", "c")


def prepare_kernel(kv_ref, wp_ref, wr_ref, ku_ref, vu_ref, kv_out, w_out):
    raw = kv_ref[...].astype(jnp.float32)
    latent = raw[:, :LATENT_WIDTH]
    energy = jnp.mean(latent * latent, axis=1, keepdims=True)
    normed = (latent * lax.rsqrt(energy + 1e-06)).astype(jnp.bfloat16)
    rope = raw[:, LATENT_WIDTH:]
    rope = jnp.concatenate([rope, jnp.zeros_like(rope)], axis=1).astype(jnp.bfloat16)
    for copy in range(kv_out.shape[0]):
        kv_out[copy, :, 0:LATENT_WIDTH] = normed
        kv_out[copy, :, LATENT_WIDTH:WIDTH] = rope
    w_out[0:96, 0:256] = wp_ref[...]
    w_out[0:96, 256:384] = wr_ref[...]
    w_out[0:32, 384:512] = ku_ref[:, 0:128]
    w_out[32:64, 384:512] = ku_ref[:, 128:256]
    w_out[64:96, 384:512] = vu_ref[:, 0:128]
    w_out[96:112, 0:128] = vu_ref[0:16, 128:256]
    w_out[96:112, 128:256] = vu_ref[16:32, 128:256]
    w_out[96:112, 256:512] = jnp.zeros((16, 256), jnp.bfloat16)


def prepare(kv_raw, wp, wr, ku, vu):
    vmem = pl.BlockSpec(memory_space=pltpu.VMEM)
    return pl.pallas_call(
        prepare_kernel,
        out_shape=(
            jax.ShapeDtypeStruct((32, 8, WIDTH), jnp.bfloat16),
            jax.ShapeDtypeStruct((112, 512), jnp.bfloat16),
        ),
        in_specs=[vmem] * 5,
        out_specs=(vmem, vmem),
    )(kv_raw, wp, wr, ku, vu)


def swap(x, axis):
    return lax.ppermute(x, axis, [(0, 1), (1, 0)])


def in_order(bit, own, other, axis):
    first = jnp.where(bit == 0, own, other)
    second = jnp.where(bit == 0, other, own)
    return jnp.concatenate([first, second], axis=axis)


def gather_direct(x, axes, members):
    return lax.all_to_all(jnp.broadcast_to(x[None], (members,) + x.shape), axes, 0, 0)


def project_kernel(core_ref, mine_ref, other_ref, w_ref, q_out, vu_out):
    def rows_of(first, many, cols):
        parts = [w_ref[:, half, first : first + many, cols] for half in range(2)]
        return [part.reshape(8 * many, part.shape[-1]) for part in parts]

    low, high = rows_of(0, 96, slice(0, 384))

    def product(ref):
        return jnp.dot(ref[:, 0:768], low, preferred_element_type=jnp.float32) + jnp.dot(
            ref[:, 768:1536], high, preferred_element_type=jnp.float32
        )

    mine, other = product(mine_ref), product(other_ref)
    is_first = core_ref[0] == 0
    parts = [jnp.where(is_first, mine, other), jnp.where(is_first, other, mine)]
    projected = jnp.stack([part.reshape(16, 8, 384) for part in parts], axis=1).reshape(256, 384)
    for head in range(2):
        nope = projected[:, head * 128 : head * 128 + 128].astype(jnp.bfloat16)
        rope = projected[:, 256 + head * 64 : 320 + head * 64]
        key_up = jnp.concatenate(rows_of(32 * head, 32, slice(384, 512)), axis=0)
        absorbed = lax.dot_general(nope, key_up, (((1,), (1,)), ((), ())), preferred_element_type=jnp.float32)
        at = pl.ds(head * 256, 256)
        q_out[at, 0:LATENT_WIDTH] = absorbed.astype(jnp.bfloat16)
        q_out[at, LATENT_WIDTH:WIDTH] = jnp.concatenate([rope, jnp.zeros_like(rope)], axis=1).astype(jnp.bfloat16)
    vu_out[:, 0:128] = jnp.concatenate(rows_of(64, 32, slice(384, 512)), axis=0)
    for half in range(2):
        upper = [w_ref[:, half, 96:112, 128 * j : 128 * j + 128] for j in range(2)]
        vu_out[pl.ds(half * 256, 256), 128:256] = jnp.concatenate(upper, axis=1).reshape(256, 128)


def project(core, mine, other, weights):
    vmem = pl.BlockSpec(memory_space=pltpu.VMEM)
    return pl.pallas_call(
        project_kernel,
        out_shape=(
            jax.ShapeDtypeStruct((512, WIDTH), jnp.bfloat16),
            jax.ShapeDtypeStruct((512, 256), jnp.bfloat16),
        ),
        in_specs=[pl.BlockSpec(memory_space=pltpu.SMEM)] + [vmem] * 3,
        out_specs=(vmem, vmem),
        compiler_params=pltpu.CompilerParams(vmem_limit_bytes=32 * 1024 * 1024),
    )(core.reshape(1), mine, other, weights)


def attend(q_ref, keys_refs, low_ref, high_ref, bounds_ref, s_ref, peaks):
    q = q_ref[...]
    rows = q.shape[0]
    steps = []
    for keys_ref in keys_refs:
        for start in range(0, keys_ref.shape[0], KEY_STEP):
            steps.append((len(steps) * KEY_STEP, keys_ref, start))
    groups = rows // TILE
    half = groups // 2
    highest = [jnp.full((TILE, 128), FLOOR, jnp.float32) for _ in range(groups)]
    for at, keys_ref, start in steps:
        keys = keys_ref[pl.ds(start, KEY_STEP), :]
        scores = lax.dot_general(
            q, keys, (((1,), (1,)), ((), ())), preferred_element_type=jnp.float32
        )
        for tile in range(half):
            last = bounds_ref[pl.ds(tile * TILE, TILE), 0:1]
            first = bounds_ref[pl.ds(tile * TILE, TILE), 1:2]
            low = low_ref[tile : tile + 1, pl.ds(at, KEY_STEP)]
            high = high_ref[tile : tile + 1, pl.ds(at, KEY_STEP)]
            allowed = (low <= last) & (high >= first)
            for head in range(2):
                g = head * half + tile
                part = jnp.where(allowed, scores[g * TILE : (g + 1) * TILE, :], NEG)
                s_ref[pl.ds(g * TILE, TILE), pl.ds(at, KEY_STEP)] = part
                top = highest[g]
                for lane in range(0, KEY_STEP, 128):
                    top = jnp.maximum(top, part[:, lane : lane + 128])
                highest[g] = top
    found = [jnp.max(h, axis=1, keepdims=True) for h in highest]
    if peaks is not None:
        found = [jnp.maximum(new, old) for new, old in zip(found, peaks)]
    sums = [jnp.zeros((TILE, 128), jnp.float32) for _ in range(groups)]
    accum = jnp.zeros((rows, LATENT_WIDTH), jnp.float32)
    for at, keys_ref, start in steps:
        parts = []
        for g in range(groups):
            part = s_ref[pl.ds(g * TILE, TILE), pl.ds(at, KEY_STEP)]
            weights = jnp.exp2((part - found[g]) * FACTOR)
            total = sums[g]
            for lane in range(0, KEY_STEP, 128):
                total = total + weights[:, lane : lane + 128]
            sums[g] = total
            parts.append(weights.astype(jnp.bfloat16))
        accum = accum + jnp.dot(
            jnp.concatenate(parts, axis=0),
            keys_ref[pl.ds(start, KEY_STEP), 0:LATENT_WIDTH],
            preferred_element_type=jnp.float32,
        )
    return [jnp.sum(s, axis=1, keepdims=True) for s in sums], found, accum


def first_half_kernel(*refs):
    q_ref, *keys_refs = refs[:-7]
    low_ref, high_ref, bounds_ref, accum_ref, sums_ref, peaks_ref, s_ref = refs[-7:]
    sums, peaks, accum = attend(q_ref, keys_refs, low_ref, high_ref, bounds_ref, s_ref, None)
    accum_ref[...] = accum
    for g in range(len(sums)):
        sums_ref[pl.ds(g * TILE, TILE), :] = jnp.broadcast_to(sums[g], (TILE, 128))
        peaks_ref[pl.ds(g * TILE, TILE), :] = jnp.broadcast_to(peaks[g], (TILE, 128))


def second_half_kernel(*refs):
    q_ref, *keys_refs = refs[:-9]
    low_ref, high_ref, bounds_ref, accum_ref, sums_ref, peaks_ref, vu_ref, o_ref, s_ref = refs[-9:]
    groups = q_ref.shape[0] // TILE
    half = groups // 2
    old = [peaks_ref[pl.ds(g * TILE, TILE), 0:1] for g in range(groups)]
    sums, peaks, accum = attend(q_ref, keys_refs, low_ref, high_ref, bounds_ref, s_ref, old)
    latent_out = []
    for g in range(groups):
        rows = pl.ds(g * TILE, TILE)
        carry = jnp.exp2((old[g] - peaks[g]) * FACTOR)
        total = sums[g] + sums_ref[rows, 0:1] * carry
        summed = accum[g * TILE : (g + 1) * TILE, :] + accum_ref[rows, :] * carry
        latent_out.append((summed * (1.0 / total)).astype(jnp.bfloat16))
    for head in range(2):
        cols = pl.ds(head * VALUE_DIMS, VALUE_DIMS)
        o_ref[:, cols] = jnp.dot(
            jnp.concatenate(latent_out[head * half : (head + 1) * half], axis=0),
            vu_ref[:, cols],
            preferred_element_type=jnp.float32,
        ).astype(jnp.bfloat16)


def attention(query, mine, theirs, low, high, bounds, value_up):
    rows, count = query.shape[0], low.shape[1] // 2
    vmem = pl.BlockSpec(memory_space=pltpu.VMEM)
    common = dict(
        scratch_shapes=[pltpu.VMEM((rows, count), jnp.float32)],
        compiler_params=pltpu.CompilerParams(vmem_limit_bytes=32 * 1024 * 1024),
        cost_estimate=pl.CostEstimate(
            flops=2 * rows * count * (576 + 512), bytes_accessed=count * WIDTH * 2, transcendentals=rows * count
        ),
    )
    state = pl.pallas_call(
        first_half_kernel,
        out_shape=(
            jax.ShapeDtypeStruct((rows, LATENT_WIDTH), jnp.float32),
            jax.ShapeDtypeStruct((rows, 128), jnp.float32),
            jax.ShapeDtypeStruct((rows, 128), jnp.float32),
        ),
        in_specs=[vmem] * (4 + len(mine)),
        out_specs=(vmem,) * 3,
        **common,
    )(query, *mine, low[:, :count], high[:, :count], bounds)
    return pl.pallas_call(
        second_half_kernel,
        out_shape=jax.ShapeDtypeStruct((rows // 2, 2 * VALUE_DIMS), jnp.bfloat16),
        in_specs=[vmem] * (8 + len(theirs)),
        out_specs=vmem,
        **common,
    )(query, *theirs, low[:, count:], high[:, count:], bounds, *state, value_up)


def body(
    q_latent,
    kv_raw,
    query_plain_weight,
    query_rotary_weight,
    key_up_weight,
    value_up_weight,
    doc_starts,
    tile_kind,
):
    xl, z2, z1 = lax.axis_index("xl"), lax.axis_index("z2"), lax.axis_index("z1")
    y1, xh, core = lax.axis_index("y1"), lax.axis_index("xh"), lax.axis_index("c")

    kv, packed = prepare(kv_raw, query_plain_weight, query_rotary_weight, key_up_weight, value_up_weight)

    kv, packed, q_latent = lax.optimization_barrier((kv, packed, q_latent))
    w_pair = in_order(xl, packed[None], swap(packed, "xl")[None], 0)
    q_pair = in_order(xh, q_latent[None], swap(q_latent, "xh")[None], 0)

    near = lax.all_to_all(kv, (*Z, "y2"), 0, 0).reshape(256, WIDTH)
    weights = lax.all_gather(w_pair, Z)

    q_pair, near = lax.optimization_barrier((q_pair, near))
    q_half = gather_direct(q_pair, ("y2", "y1"), 8)
    q_core = swap(q_half, "c")

    next_y = swap(near, "y1")
    x2_near = swap(near, "xh")
    pair = jnp.concatenate([near, next_y], axis=0)
    x1_pair = swap(pair, "xl")
    x3_pair = lax.ppermute(pair, ("xl", "xh"), [(0, 3), (3, 0), (1, 2), (2, 1)])
    x2_far, pair = lax.optimization_barrier((x2_near, pair))
    x2_next = swap(x2_far, "y1")
    x2_pair = jnp.concatenate([x2_near, x2_next], axis=0)

    query, value_up = project(core, q_half.reshape(128, 1536), q_core.reshape(128, 1536), weights)

    x1_pair, x3_pair, query = lax.optimization_barrier((x1_pair, x3_pair, query))
    mine = [pair, x1_pair, x2_pair, x3_pair]
    theirs = [swap(piece, "c") for piece in mine]

    shape = (2, 4, 2, 8, 4, 8)
    at = lambda d: lax.broadcasted_iota(jnp.int32, shape, d)
    far = at(1)
    k_xl, k_xh = xl ^ (far & 1), xh ^ (far >> 1)
    k_block = k_xl * 8 + at(3)
    k_y = 2 * at(4) + (y1 ^ at(2))
    k_pos = (k_block * 256 + ((k_y * 2 + k_xh) * 2 + (core ^ at(0))) * 8 + at(5)).reshape(1, 4096)
    k_tile = k_pos // TILE
    kinds = jnp.sum(
        jnp.where(
            lax.broadcasted_iota(jnp.int32, (1, 32, 4096), 1) == k_tile[:, None, :], tile_kind[:, :, None], 0
        ),
        axis=1,
    )
    big = jnp.int32(1 << 20)
    low = jnp.where(kinds == 2, k_pos, jnp.where(kinds == 1, -1, big))
    high = jnp.where(kinds == 2, k_pos, jnp.where(kinds == 1, big, -1))
    q_pos = (xl * 8 + 2 * z2 + z1) * 256 + lax.broadcasted_iota(jnp.int32, (256, 1), 0)
    q_first = jnp.max(jnp.where(doc_starts[None, :] <= q_pos, doc_starts[None, :], 0), axis=1, keepdims=True)
    bounds = jnp.concatenate([q_pos, q_first], axis=1)
    return attention(query, mine, theirs, low, high, bounds, value_up)


def solution(mesh):
    fine = Mesh(np.asarray(mesh.devices).reshape(SIZES), AXES)
    return jax.shard_map(
        body,
        mesh=fine,
        in_specs=(
            P(AXES, None),
            P(AXES, None),
            P(BLK, WIDE),
            P(BLK, WIDE),
            P(BLK, WIDE),
            P(BLK, WIDE),
            P(),
            P(BLK, None),
        ),
        out_specs=P(BLK, WIDE),
        check_vma=False,
    )
```

```python
import jax
import jax.numpy as jnp
import numpy as np
from jax import lax
from jax.experimental import pallas as pl
from jax.experimental.pallas import tpu as pltpu
from jax.sharding import Mesh, PartitionSpec as P

LATENT_WIDTH = 512
ROTARY_DIMS = 64
PLAIN_QUERY_DIMS = 128
VALUE_DIMS = 128
TILE = 128
WIDTH = 640
KEY_STEP = 512
SCALE = (PLAIN_QUERY_DIMS + ROTARY_DIMS) ** (-0.5)
FACTOR = SCALE * 1.4426950408889634
NEG = -1e30
FLOOR = -1e29

AXES = ("xl", "z2", "z1", "y2", "y1", "xh", "c")
SIZES = (2, 4, 2, 4, 2, 2, 2)
Z = ("z2", "z1")
BLK = ("xl", "z2", "z1")
WIDE = ("y2", "y1", "xh", "c")


def prepare_kernel(kv_ref, wp_ref, wr_ref, ku_ref, vu_ref, kv_out, w_out):
    raw = kv_ref[...].astype(jnp.float32)
    latent = raw[:, :LATENT_WIDTH]
    energy = jnp.mean(latent * latent, axis=1, keepdims=True)
    normed = (latent * lax.rsqrt(energy + 1e-06)).astype(jnp.bfloat16)
    rope = raw[:, LATENT_WIDTH:]
    rope = jnp.concatenate([rope, jnp.zeros_like(rope)], axis=1).astype(jnp.bfloat16)
    for copy in range(kv_out.shape[0]):
        kv_out[copy, :, 0:LATENT_WIDTH] = normed
        kv_out[copy, :, LATENT_WIDTH:WIDTH] = rope
    w_out[0:96, 0:256] = wp_ref[...]
    w_out[0:96, 256:384] = wr_ref[...]
    w_out[0:32, 384:512] = ku_ref[:, 0:128]
    w_out[32:64, 384:512] = ku_ref[:, 128:256]
    w_out[64:96, 384:512] = vu_ref[:, 0:128]
    w_out[96:112, 0:128] = vu_ref[0:16, 128:256]
    w_out[96:112, 128:256] = vu_ref[16:32, 128:256]
    w_out[96:112, 256:512] = jnp.zeros((16, 256), jnp.bfloat16)


def prepare(kv_raw, wp, wr, ku, vu):
    vmem = pl.BlockSpec(memory_space=pltpu.VMEM)
    return pl.pallas_call(
        prepare_kernel,
        out_shape=(
            jax.ShapeDtypeStruct((32, 8, WIDTH), jnp.bfloat16),
            jax.ShapeDtypeStruct((112, 512), jnp.bfloat16),
        ),
        in_specs=[vmem] * 5,
        out_specs=(vmem, vmem),
    )(kv_raw, wp, wr, ku, vu)


def swap(x, axis):
    return lax.ppermute(x, axis, [(0, 1), (1, 0)])


def in_order(bit, own, other, axis):
    first = jnp.where(bit == 0, own, other)
    second = jnp.where(bit == 0, other, own)
    return jnp.concatenate([first, second], axis=axis)


def gather_direct(x, axes, members):
    return lax.all_to_all(jnp.broadcast_to(x[None], (members,) + x.shape), axes, 0, 0)


def project_kernel(core_ref, mine_ref, other_ref, w_ref, q_out, vu_out):
    def rows_of(first, many, cols):
        parts = [w_ref[:, half, first : first + many, cols] for half in range(2)]
        return [part.reshape(8 * many, part.shape[-1]) for part in parts]

    low, high = rows_of(0, 96, slice(0, 384))

    def product(ref):
        return jnp.dot(ref[:, 0:768], low, preferred_element_type=jnp.float32) + jnp.dot(
            ref[:, 768:1536], high, preferred_element_type=jnp.float32
        )

    mine, other = product(mine_ref), product(other_ref)
    is_first = core_ref[0] == 0
    parts = [jnp.where(is_first, mine, other), jnp.where(is_first, other, mine)]
    projected = jnp.stack([part.reshape(16, 8, 384) for part in parts], axis=1).reshape(256, 384)
    for head in range(2):
        nope = projected[:, head * 128 : head * 128 + 128].astype(jnp.bfloat16)
        rope = projected[:, 256 + head * 64 : 320 + head * 64]
        key_up = jnp.concatenate(rows_of(32 * head, 32, slice(384, 512)), axis=0)
        absorbed = lax.dot_general(nope, key_up, (((1,), (1,)), ((), ())), preferred_element_type=jnp.float32)
        at = pl.ds(head * 256, 256)
        q_out[at, 0:LATENT_WIDTH] = absorbed.astype(jnp.bfloat16)
        q_out[at, LATENT_WIDTH:WIDTH] = jnp.concatenate([rope, jnp.zeros_like(rope)], axis=1).astype(jnp.bfloat16)
    vu_out[:, 0:128] = jnp.concatenate(rows_of(64, 32, slice(384, 512)), axis=0)
    for half in range(2):
        upper = [w_ref[:, half, 96:112, 128 * j : 128 * j + 128] for j in range(2)]
        vu_out[pl.ds(half * 256, 256), 128:256] = jnp.concatenate(upper, axis=1).reshape(256, 128)


def project(core, mine, other, weights):
    vmem = pl.BlockSpec(memory_space=pltpu.VMEM)
    return pl.pallas_call(
        project_kernel,
        out_shape=(
            jax.ShapeDtypeStruct((512, WIDTH), jnp.bfloat16),
            jax.ShapeDtypeStruct((512, 256), jnp.bfloat16),
        ),
        in_specs=[pl.BlockSpec(memory_space=pltpu.SMEM)] + [vmem] * 3,
        out_specs=(vmem, vmem),
        compiler_params=pltpu.CompilerParams(vmem_limit_bytes=32 * 1024 * 1024),
    )(core.reshape(1), mine, other, weights)


def attend(q_ref, keys_refs, low_ref, high_ref, bounds_ref, s_ref, peaks):
    q = q_ref[...]
    rows = q.shape[0]
    steps = []
    for keys_ref in keys_refs:
        for start in range(0, keys_ref.shape[0], KEY_STEP):
            steps.append((len(steps) * KEY_STEP, keys_ref, start))
    groups = rows // TILE
    half = groups // 2
    highest = [jnp.full((TILE, 128), FLOOR, jnp.float32) for _ in range(groups)]
    for at, keys_ref, start in steps:
        keys = keys_ref[pl.ds(start, KEY_STEP), :]
        scores = lax.dot_general(
            q, keys, (((1,), (1,)), ((), ())), preferred_element_type=jnp.float32
        )
        for tile in range(half):
            last = bounds_ref[pl.ds(tile * TILE, TILE), 0:1]
            first = bounds_ref[pl.ds(tile * TILE, TILE), 1:2]
            low = low_ref[tile : tile + 1, pl.ds(at, KEY_STEP)]
            high = high_ref[tile : tile + 1, pl.ds(at, KEY_STEP)]
            allowed = (low <= last) & (high >= first)
            for head in range(2):
                g = head * half + tile
                part = jnp.where(allowed, scores[g * TILE : (g + 1) * TILE, :], NEG)
                s_ref[pl.ds(g * TILE, TILE), pl.ds(at, KEY_STEP)] = part
                top = highest[g]
                for lane in range(0, KEY_STEP, 128):
                    top = jnp.maximum(top, part[:, lane : lane + 128])
                highest[g] = top
    found = [jnp.max(h, axis=1, keepdims=True) for h in highest]
    if peaks is not None:
        found = [jnp.maximum(new, old) for new, old in zip(found, peaks)]
    sums = [jnp.zeros((TILE, 128), jnp.float32) for _ in range(groups)]
    accum = jnp.zeros((rows, LATENT_WIDTH), jnp.float32)
    for at, keys_ref, start in steps:
        parts = []
        for g in range(groups):
            part = s_ref[pl.ds(g * TILE, TILE), pl.ds(at, KEY_STEP)]
            weights = jnp.exp2((part - found[g]) * FACTOR)
            total = sums[g]
            for lane in range(0, KEY_STEP, 128):
                total = total + weights[:, lane : lane + 128]
            sums[g] = total
            parts.append(weights.astype(jnp.bfloat16))
        accum = accum + jnp.dot(
            jnp.concatenate(parts, axis=0),
            keys_ref[pl.ds(start, KEY_STEP), 0:LATENT_WIDTH],
            preferred_element_type=jnp.float32,
        )
    return [jnp.sum(s, axis=1, keepdims=True) for s in sums], found, accum


def first_half_kernel(*refs):
    q_ref, *keys_refs = refs[:-7]
    low_ref, high_ref, bounds_ref, accum_ref, sums_ref, peaks_ref, s_ref = refs[-7:]
    sums, peaks, accum = attend(q_ref, keys_refs, low_ref, high_ref, bounds_ref, s_ref, None)
    accum_ref[...] = accum
    for g in range(len(sums)):
        sums_ref[pl.ds(g * TILE, TILE), :] = jnp.broadcast_to(sums[g], (TILE, 128))
        peaks_ref[pl.ds(g * TILE, TILE), :] = jnp.broadcast_to(peaks[g], (TILE, 128))


def second_half_kernel(*refs):
    q_ref, *keys_refs = refs[:-9]
    low_ref, high_ref, bounds_ref, accum_ref, sums_ref, peaks_ref, vu_ref, o_ref, s_ref = refs[-9:]
    groups = q_ref.shape[0] // TILE
    half = groups // 2
    old = [peaks_ref[pl.ds(g * TILE, TILE), 0:1] for g in range(groups)]
    sums, peaks, accum = attend(q_ref, keys_refs, low_ref, high_ref, bounds_ref, s_ref, old)
    latent_out = []
    for g in range(groups):
        rows = pl.ds(g * TILE, TILE)
        carry = jnp.exp2((old[g] - peaks[g]) * FACTOR)
        total = sums[g] + sums_ref[rows, 0:1] * carry
        summed = accum[g * TILE : (g + 1) * TILE, :] + accum_ref[rows, :] * carry
        latent_out.append((summed * (1.0 / total)).astype(jnp.bfloat16))
    for head in range(2):
        cols = pl.ds(head * VALUE_DIMS, VALUE_DIMS)
        o_ref[:, cols] = jnp.dot(
            jnp.concatenate(latent_out[head * half : (head + 1) * half], axis=0),
            vu_ref[:, cols],
            preferred_element_type=jnp.float32,
        ).astype(jnp.bfloat16)


def attention(query, mine, theirs, low, high, bounds, value_up):
    rows, count = query.shape[0], low.shape[1] // 2
    vmem = pl.BlockSpec(memory_space=pltpu.VMEM)
    common = dict(
        scratch_shapes=[pltpu.VMEM((rows, count), jnp.float32)],
        compiler_params=pltpu.CompilerParams(vmem_limit_bytes=32 * 1024 * 1024),
        cost_estimate=pl.CostEstimate(
            flops=2 * rows * count * (576 + 512), bytes_accessed=count * WIDTH * 2, transcendentals=rows * count
        ),
    )
    state = pl.pallas_call(
        first_half_kernel,
        out_shape=(
            jax.ShapeDtypeStruct((rows, LATENT_WIDTH), jnp.float32),
            jax.ShapeDtypeStruct((rows, 128), jnp.float32),
            jax.ShapeDtypeStruct((rows, 128), jnp.float32),
        ),
        in_specs=[vmem] * (4 + len(mine)),
        out_specs=(vmem,) * 3,
        **common,
    )(query, *mine, low[:, :count], high[:, :count], bounds)
    return pl.pallas_call(
        second_half_kernel,
        out_shape=jax.ShapeDtypeStruct((rows // 2, 2 * VALUE_DIMS), jnp.bfloat16),
        in_specs=[vmem] * (8 + len(theirs)),
        out_specs=vmem,
        **common,
    )(query, *theirs, low[:, count:], high[:, count:], bounds, *state, value_up)


def body(
    q_latent,
    kv_raw,
    query_plain_weight,
    query_rotary_weight,
    key_up_weight,
    value_up_weight,
    doc_starts,
    tile_kind,
):
    xl, z2, z1 = lax.axis_index("xl"), lax.axis_index("z2"), lax.axis_index("z1")
    y1, xh, core = lax.axis_index("y1"), lax.axis_index("xh"), lax.axis_index("c")

    kv, packed = prepare(kv_raw, query_plain_weight, query_rotary_weight, key_up_weight, value_up_weight)

    kv, packed, q_latent = lax.optimization_barrier((kv, packed, q_latent))
    w_pair = in_order(xl, packed[None], swap(packed, "xl")[None], 0)
    q_pair = in_order(xh, q_latent[None], swap(q_latent, "xh")[None], 0)

    near = lax.all_to_all(kv, (*Z, "y2"), 0, 0).reshape(256, WIDTH)
    weights = lax.all_gather(w_pair, Z)

    q_pair, near = lax.optimization_barrier((q_pair, near))
    q_half = gather_direct(q_pair, ("y2", "y1"), 8)
    q_core = swap(q_half, "c")

    next_y = swap(near, "y1")
    x2_near = swap(near, "xh")
    pair = jnp.concatenate([near, next_y], axis=0)
    x1_pair = swap(pair, "xl")
    x3_pair = lax.ppermute(pair, ("xl", "xh"), [(0, 3), (3, 0), (1, 2), (2, 1)])
    x2_far, pair = lax.optimization_barrier((x2_near, pair))
    x2_next = swap(x2_far, "y1")
    x2_pair = jnp.concatenate([x2_near, x2_next], axis=0)

    query, value_up = project(core, q_half.reshape(128, 1536), q_core.reshape(128, 1536), weights)

    mine = [pair, x1_pair, x2_pair, x3_pair]
    theirs = [swap(piece, "c") for piece in mine]

    shape = (2, 4, 2, 8, 4, 8)
    at = lambda d: lax.broadcasted_iota(jnp.int32, shape, d)
    far = at(1)
    k_xl, k_xh = xl ^ (far & 1), xh ^ (far >> 1)
    k_block = k_xl * 8 + at(3)
    k_y = 2 * at(4) + (y1 ^ at(2))
    k_pos = (k_block * 256 + ((k_y * 2 + k_xh) * 2 + (core ^ at(0))) * 8 + at(5)).reshape(1, 4096)
    k_tile = k_pos // TILE
    kinds = jnp.sum(
        jnp.where(
            lax.broadcasted_iota(jnp.int32, (1, 32, 4096), 1) == k_tile[:, None, :], tile_kind[:, :, None], 0
        ),
        axis=1,
    )
    big = jnp.int32(1 << 20)
    low = jnp.where(kinds == 2, k_pos, jnp.where(kinds == 1, -1, big))
    high = jnp.where(kinds == 2, k_pos, jnp.where(kinds == 1, big, -1))
    q_pos = (xl * 8 + 2 * z2 + z1) * 256 + lax.broadcasted_iota(jnp.int32, (256, 1), 0)
    q_first = jnp.max(jnp.where(doc_starts[None, :] <= q_pos, doc_starts[None, :], 0), axis=1, keepdims=True)
    bounds = jnp.concatenate([q_pos, q_first], axis=1)
    return attention(query, mine, theirs, low, high, bounds, value_up)


def solution(mesh):
    fine = Mesh(np.asarray(mesh.devices).reshape(SIZES), AXES)
    return jax.shard_map(
        body,
        mesh=fine,
        in_specs=(
            P(AXES, None),
            P(AXES, None),
            P(BLK, WIDE),
            P(BLK, WIDE),
            P(BLK, WIDE),
            P(BLK, WIDE),
            P(),
            P(BLK, None),
        ),
        out_specs=P(BLK, WIDE),
        check_vma=False,
    )
```

```python
import jax
import jax.numpy as jnp
import numpy as np
from jax import lax
from jax.experimental import pallas as pl
from jax.experimental.pallas import tpu as pltpu
from jax.sharding import Mesh, PartitionSpec as P

LATENT_WIDTH = 512
ROTARY_DIMS = 64
PLAIN_QUERY_DIMS = 128
VALUE_DIMS = 128
TILE = 128
WIDTH = 640
PROJECT_COST = 5_000_000_000
SCALE = (PLAIN_QUERY_DIMS + ROTARY_DIMS) ** (-0.5)
FACTOR = SCALE * 1.4426950408889634
NEG = -1e30
FLOOR = -1e29

AXES = ("xl", "z2", "z1", "y2", "y1", "xh", "c")
SIZES = (2, 4, 2, 4, 2, 2, 2)
Z = ("z2", "z1")
BLK = ("xl", "z2", "z1")
WIDE = ("y2", "y1", "xh", "c")


def prepare_kernel(kv_ref, wp_ref, wr_ref, ku_ref, vu_ref, kv_out, w_out):
    raw = kv_ref[...].astype(jnp.float32)
    latent = raw[:, :LATENT_WIDTH]
    energy = jnp.mean(latent * latent, axis=1, keepdims=True)
    normed = (latent * lax.rsqrt(energy + 1e-06)).astype(jnp.bfloat16)
    rope = raw[:, LATENT_WIDTH:]
    rope = jnp.concatenate([rope, jnp.zeros_like(rope)], axis=1).astype(jnp.bfloat16)
    for copy in range(kv_out.shape[0]):
        kv_out[copy, :, 0:LATENT_WIDTH] = normed
        kv_out[copy, :, LATENT_WIDTH:WIDTH] = rope
    w_out[0:96, 0:256] = wp_ref[...]
    w_out[0:96, 256:384] = wr_ref[...]
    w_out[0:32, 384:512] = ku_ref[:, 0:128]
    w_out[32:64, 384:512] = ku_ref[:, 128:256]
    w_out[64:96, 384:512] = vu_ref[:, 0:128]
    w_out[96:112, 0:128] = vu_ref[0:16, 128:256]
    w_out[96:112, 128:256] = vu_ref[16:32, 128:256]
    w_out[96:112, 256:512] = jnp.zeros((16, 256), jnp.bfloat16)


def prepare(kv_raw, wp, wr, ku, vu):
    vmem = pl.BlockSpec(memory_space=pltpu.VMEM)
    return pl.pallas_call(
        prepare_kernel,
        out_shape=(
            jax.ShapeDtypeStruct((32, 8, WIDTH), jnp.bfloat16),
            jax.ShapeDtypeStruct((112, 512), jnp.bfloat16),
        ),
        in_specs=[vmem] * 5,
        out_specs=(vmem, vmem),
    )(kv_raw, wp, wr, ku, vu)


def swap(x, axis):
    return lax.ppermute(x, axis, [(0, 1), (1, 0)])


def in_order(bit, own, other, axis):
    first = jnp.where(bit == 0, own, other)
    second = jnp.where(bit == 0, other, own)
    return jnp.concatenate([first, second], axis=axis)


def gather_direct(x, axes, members):
    return lax.all_to_all(jnp.broadcast_to(x[None], (members,) + x.shape), axes, 0, 0)


def project_kernel(place_ref, mine_ref, other_ref, w_ref, q_out, vu_out):
    x_lo = place_ref[1]
    half_at = [x_lo, 1 - x_lo]

    def rows_of(first, many, cols):
        parts = [w_ref[:, pl.ds(at, 1), first : first + many, cols] for at in half_at]
        return [part.reshape(8 * many, part.shape[-1]) for part in parts]

    low, high = rows_of(0, 96, slice(0, 384))

    def product(ref):
        return jnp.dot(ref[:, 0:768], low, preferred_element_type=jnp.float32) + jnp.dot(
            ref[:, 768:1536], high, preferred_element_type=jnp.float32
        )

    mine, other = product(mine_ref), product(other_ref)
    is_first = place_ref[0] == 0
    parts = [jnp.where(is_first, mine, other), jnp.where(is_first, other, mine)]
    projected = jnp.stack([part.reshape(16, 8, 384) for part in parts], axis=1).reshape(256, 384)
    for head in range(2):
        nope = projected[:, head * 128 : head * 128 + 128].astype(jnp.bfloat16)
        rope = projected[:, 256 + head * 64 : 320 + head * 64]
        key_up = jnp.concatenate(rows_of(32 * head, 32, slice(384, 512)), axis=0)
        absorbed = lax.dot_general(nope, key_up, (((1,), (1,)), ((), ())), preferred_element_type=jnp.float32)
        at = pl.ds(head * 256, 256)
        q_out[at, 0:LATENT_WIDTH] = absorbed.astype(jnp.bfloat16)
        q_out[at, LATENT_WIDTH:WIDTH] = jnp.concatenate([rope, jnp.zeros_like(rope)], axis=1).astype(jnp.bfloat16)
    vu_out[:, 0:128] = jnp.concatenate(rows_of(64, 32, slice(384, 512)), axis=0)
    for half in range(2):
        upper = [w_ref[:, pl.ds(half_at[half], 1), 96:112, 128 * j : 128 * j + 128] for j in range(2)]
        vu_out[pl.ds(half * 256, 256), 128:256] = jnp.concatenate(upper, axis=2).reshape(256, 128)


def project(place, mine, other, weights):
    vmem = pl.BlockSpec(memory_space=pltpu.VMEM)
    return pl.pallas_call(
        project_kernel,
        out_shape=(
            jax.ShapeDtypeStruct((4 * mine.shape[0], WIDTH), jnp.bfloat16),
            jax.ShapeDtypeStruct((LATENT_WIDTH, 2 * VALUE_DIMS), jnp.bfloat16),
        ),
        in_specs=[pl.BlockSpec(memory_space=pltpu.SMEM)] + [vmem] * 3,
        out_specs=(vmem, vmem),
        compiler_params=pltpu.CompilerParams(vmem_limit_bytes=16 * 1024 * 1024),
        cost_estimate=pl.CostEstimate(flops=PROJECT_COST, bytes_accessed=0, transcendentals=0),
    )(place, mine, other, weights)


def attention_kernel(q_ref, vu_ref, low_ref, high_ref, bounds_ref, *refs):
    pieces, (o_ref, keys_ref, s_ref, sems) = refs[:-4], refs[-4:]
    step, many = pieces[0].shape[0], len(pieces) // 2
    fetches = []
    for i, piece in enumerate(pieces):
        fetches.append(pltpu.make_async_copy(piece, keys_ref.at[pl.ds(i * step, step), :], sems.at[i]))
        fetches[-1].start()
    q = q_ref[...]
    rows = q.shape[0]
    groups = rows // TILE
    half = groups // 2
    peaks = [jnp.full((TILE, 1), FLOOR, jnp.float32) for _ in range(groups)]
    totals = [jnp.zeros((TILE, 1), jnp.float32) for _ in range(groups)]
    summed = None
    for turn in range(2):
        for fetch in fetches[turn * many : (turn + 1) * many]:
            fetch.wait()
        highest = [jnp.full((TILE, 128), FLOOR, jnp.float32) for _ in range(groups)]
        for i in range(many):
            at = pl.ds((turn * many + i) * step, step)
            scores = lax.dot_general(
                q, keys_ref[at, :], (((1,), (1,)), ((), ())), preferred_element_type=jnp.float32
            )
            for tile in range(half):
                last = bounds_ref[pl.ds(tile * TILE, TILE), 0:1]
                first = bounds_ref[pl.ds(tile * TILE, TILE), 1:2]
                allowed = (low_ref[tile : tile + 1, at] <= last) & (high_ref[tile : tile + 1, at] >= first)
                for head in range(2):
                    g = head * half + tile
                    part = jnp.where(allowed, scores[g * TILE : (g + 1) * TILE, :], NEG)
                    s_ref[pl.ds(g * TILE, TILE), pl.ds(i * step, step)] = part
                    for lane in range(0, step, 128):
                        highest[g] = jnp.maximum(highest[g], part[:, lane : lane + 128])
        old = peaks
        peaks = [jnp.maximum(p, jnp.max(h, axis=1, keepdims=True)) for p, h in zip(old, highest)]
        sums = [jnp.zeros((TILE, 128), jnp.float32) for _ in range(groups)]
        accum = jnp.zeros((rows, LATENT_WIDTH), jnp.float32)
        for i in range(many):
            parts = []
            for g in range(groups):
                weights = jnp.exp2((s_ref[pl.ds(g * TILE, TILE), pl.ds(i * step, step)] - peaks[g]) * FACTOR)
                for lane in range(0, step, 128):
                    sums[g] = sums[g] + weights[:, lane : lane + 128]
                parts.append(weights.astype(jnp.bfloat16))
            accum = accum + jnp.dot(
                jnp.concatenate(parts, axis=0),
                keys_ref[pl.ds((turn * many + i) * step, step), 0:LATENT_WIDTH],
                preferred_element_type=jnp.float32,
            )
        sums = [jnp.sum(total, axis=1, keepdims=True) for total in sums]
        if summed is None:
            totals, summed = sums, accum
        else:
            carry = [jnp.exp2((p - new) * FACTOR) for p, new in zip(old, peaks)]
            totals = [new + total * c for new, total, c in zip(sums, totals, carry)]
            summed = accum + summed * jnp.concatenate(carry, axis=0)
    latent_out = (summed * (1.0 / jnp.concatenate(totals, axis=0))).astype(jnp.bfloat16)
    for head in range(2):
        cols = pl.ds(head * VALUE_DIMS, VALUE_DIMS)
        o_ref[:, cols] = jnp.dot(
            latent_out[head * (rows // 2) : (head + 1) * (rows // 2), :],
            vu_ref[:, cols],
            preferred_element_type=jnp.float32,
        ).astype(jnp.bfloat16)


def attention(query, value_up, pieces, low, high, bounds):
    tokens, count = query.shape[0] // 2, low.shape[1]
    vmem, hbm = pl.BlockSpec(memory_space=pltpu.VMEM), pl.BlockSpec(memory_space=pltpu.HBM)
    return pl.pallas_call(
        attention_kernel,
        out_shape=jax.ShapeDtypeStruct((tokens, 2 * VALUE_DIMS), jnp.bfloat16),
        in_specs=[vmem] * 5 + [hbm] * len(pieces),
        out_specs=vmem,
        scratch_shapes=[
            pltpu.VMEM((count, WIDTH), jnp.bfloat16),
            pltpu.VMEM((2 * tokens, count // 2), jnp.float32),
            pltpu.SemaphoreType.DMA((len(pieces),)),
        ],
        compiler_params=pltpu.CompilerParams(vmem_limit_bytes=40 * 1024 * 1024),
        cost_estimate=pl.CostEstimate(
            flops=4 * tokens * count * (576 + 512),
            bytes_accessed=count * WIDTH * 2,
            transcendentals=2 * tokens * count,
        ),
    )(query, value_up, low, high, bounds, *pieces)


def body(
    q_latent,
    kv_raw,
    query_plain_weight,
    query_rotary_weight,
    key_up_weight,
    value_up_weight,
    doc_starts,
    tile_kind,
):
    xl, z2, z1 = lax.axis_index("xl"), lax.axis_index("z2"), lax.axis_index("z1")
    y1, xh, core = lax.axis_index("y1"), lax.axis_index("xh"), lax.axis_index("c")

    kv, packed = prepare(kv_raw, query_plain_weight, query_rotary_weight, key_up_weight, value_up_weight)

    kv, packed = lax.optimization_barrier((kv, packed))
    w_pair = jnp.stack([packed, swap(packed, "xl")], axis=0)

    near = lax.all_to_all(kv, (*Z, "y2"), 0, 0).reshape(256, WIDTH)
    weights = lax.all_gather(w_pair, Z)

    q_latent, _ = lax.optimization_barrier((q_latent, near))
    q_half = gather_direct(q_latent, ("y2", "y1", "xh"), 16)
    q_core = swap(q_half, "c")

    next_y = swap(near, "y1")
    x2_near = swap(near, "xh")
    pair = jnp.concatenate([near, next_y], axis=0)
    x1_pair = swap(pair, "xl")
    x3_pair = lax.ppermute(pair, ("xl", "xh"), [(0, 3), (3, 0), (1, 2), (2, 1)])
    x2_far, pair = lax.optimization_barrier((x2_near, pair))
    x2_next = swap(x2_far, "y1")
    x2_pair = jnp.concatenate([x2_near, x2_next], axis=0)

    mine = [pair, x1_pair, x2_pair, x3_pair]
    theirs = [swap(piece, "c") for piece in mine]

    shape = (2, 4, 2, 8, 4, 8)
    at = lambda d: lax.broadcasted_iota(jnp.int32, shape, d)
    far = at(1)
    k_xl, k_xh = xl ^ (far & 1), xh ^ (far >> 1)
    k_block = k_xl * 8 + at(3)
    k_y = 2 * at(4) + (y1 ^ at(2))
    k_pos = (k_block * 256 + ((k_y * 2 + k_xh) * 2 + (core ^ at(0))) * 8 + at(5)).reshape(1, 4096)
    k_tile = k_pos // TILE
    kinds = jnp.sum(
        jnp.where(
            lax.broadcasted_iota(jnp.int32, (1, 32, 4096), 1) == k_tile[:, None, :], tile_kind[:, :, None], 0
        ),
        axis=1,
    )
    big = jnp.int32(1 << 20)
    low = jnp.where(kinds == 2, k_pos, jnp.where(kinds == 1, -1, big))
    high = jnp.where(kinds == 2, k_pos, jnp.where(kinds == 1, big, -1))
    q_pos = (xl * 8 + 2 * z2 + z1) * 256 + lax.broadcasted_iota(jnp.int32, (256, 1), 0)
    q_first = jnp.max(jnp.where(doc_starts[None, :] <= q_pos, doc_starts[None, :], 0), axis=1, keepdims=True)
    bounds = jnp.concatenate([q_pos, q_first], axis=1)
    place = jnp.stack([core, xl])
    query, value_up = project(place, q_half.reshape(128, 1536), q_core.reshape(128, 1536), weights)
    return attention(query, value_up, mine + theirs, low, high, bounds)


def solution(mesh):
    fine = Mesh(np.asarray(mesh.devices).reshape(SIZES), AXES)
    return jax.shard_map(
        body,
        mesh=fine,
        in_specs=(
            P(AXES, None),
            P(AXES, None),
            P(BLK, WIDE),
            P(BLK, WIDE),
            P(BLK, WIDE),
            P(BLK, WIDE),
            P(),
            P(BLK, None),
        ),
        out_specs=P(BLK, WIDE),
        check_vma=False,
    )
```

```python
import jax
import jax.numpy as jnp
import numpy as np
from jax import lax
from jax.experimental import pallas as pl
from jax.experimental.pallas import tpu as pltpu
from jax.sharding import Mesh, PartitionSpec as P

LATENT_WIDTH = 512
ROTARY_DIMS = 64
PLAIN_QUERY_DIMS = 128
VALUE_DIMS = 128
TILE = 128
WIDTH = 640
PROJECT_COST = 5_000_000_000
SCALE = (PLAIN_QUERY_DIMS + ROTARY_DIMS) ** (-0.5)
FACTOR = SCALE * 1.4426950408889634
NEG = -1e30
FLOOR = -1e29

AXES = ("xl", "z2", "z1", "y2", "y1", "xh", "c")
SIZES = (2, 4, 2, 4, 2, 2, 2)
Z = ("z2", "z1")
BLK = ("xl", "z2", "z1")
WIDE = ("y2", "y1", "xh", "c")


def prepare_kernel(kv_ref, wp_ref, wr_ref, ku_ref, vu_ref, kv_out, w_out):
    raw = kv_ref[...].astype(jnp.float32)
    latent = raw[:, :LATENT_WIDTH]
    energy = jnp.mean(latent * latent, axis=1, keepdims=True)
    normed = (latent * lax.rsqrt(energy + 1e-06)).astype(jnp.bfloat16)
    rope = raw[:, LATENT_WIDTH:]
    rope = jnp.concatenate([rope, jnp.zeros_like(rope)], axis=1).astype(jnp.bfloat16)
    for copy in range(kv_out.shape[0]):
        kv_out[copy, :, 0:LATENT_WIDTH] = normed
        kv_out[copy, :, LATENT_WIDTH:WIDTH] = rope
    w_out[0:96, 0:256] = wp_ref[...]
    w_out[0:96, 256:384] = wr_ref[...]
    w_out[0:32, 384:512] = ku_ref[:, 0:128]
    w_out[32:64, 384:512] = ku_ref[:, 128:256]
    w_out[64:96, 384:512] = vu_ref[:, 0:128]
    w_out[96:112, 0:128] = vu_ref[0:16, 128:256]
    w_out[96:112, 128:256] = vu_ref[16:32, 128:256]
    w_out[96:112, 256:512] = jnp.zeros((16, 256), jnp.bfloat16)


def prepare(kv_raw, wp, wr, ku, vu):
    vmem = pl.BlockSpec(memory_space=pltpu.VMEM)
    return pl.pallas_call(
        prepare_kernel,
        out_shape=(
            jax.ShapeDtypeStruct((32, 8, WIDTH), jnp.bfloat16),
            jax.ShapeDtypeStruct((112, 512), jnp.bfloat16),
        ),
        in_specs=[vmem] * 5,
        out_specs=(vmem, vmem),
    )(kv_raw, wp, wr, ku, vu)


def swap(x, axis):
    return lax.ppermute(x, axis, [(0, 1), (1, 0)])


def in_order(bit, own, other, axis):
    first = jnp.where(bit == 0, own, other)
    second = jnp.where(bit == 0, other, own)
    return jnp.concatenate([first, second], axis=axis)


def gather_direct(x, axes, members):
    return lax.all_to_all(jnp.broadcast_to(x[None], (members,) + x.shape), axes, 0, 0)


def project_kernel(place_ref, mine_ref, other_ref, w_ref, q_out, vu_out):
    x_lo = place_ref[1]
    half_at = [x_lo, 1 - x_lo]

    def rows_of(first, many, cols):
        parts = [w_ref[:, pl.ds(at, 1), first : first + many, cols] for at in half_at]
        return [part.reshape(8 * many, part.shape[-1]) for part in parts]

    low, high = rows_of(0, 96, slice(0, 384))

    def product(ref):
        return jnp.dot(ref[:, 0:768], low, preferred_element_type=jnp.float32) + jnp.dot(
            ref[:, 768:1536], high, preferred_element_type=jnp.float32
        )

    mine, other = product(mine_ref), product(other_ref)
    is_first = place_ref[0] == 0
    parts = [jnp.where(is_first, mine, other), jnp.where(is_first, other, mine)]
    projected = jnp.stack([part.reshape(16, 8, 384) for part in parts], axis=1).reshape(256, 384)
    for head in range(2):
        nope = projected[:, head * 128 : head * 128 + 128].astype(jnp.bfloat16)
        rope = projected[:, 256 + head * 64 : 320 + head * 64]
        key_up = jnp.concatenate(rows_of(32 * head, 32, slice(384, 512)), axis=0)
        absorbed = lax.dot_general(nope, key_up, (((1,), (1,)), ((), ())), preferred_element_type=jnp.float32)
        at = pl.ds(head * 256, 256)
        q_out[at, 0:LATENT_WIDTH] = absorbed.astype(jnp.bfloat16)
        q_out[at, LATENT_WIDTH:WIDTH] = jnp.concatenate([rope, jnp.zeros_like(rope)], axis=1).astype(jnp.bfloat16)
    vu_out[:, 0:128] = jnp.concatenate(rows_of(64, 32, slice(384, 512)), axis=0)
    for half in range(2):
        upper = [w_ref[:, pl.ds(half_at[half], 1), 96:112, 128 * j : 128 * j + 128] for j in range(2)]
        vu_out[pl.ds(half * 256, 256), 128:256] = jnp.concatenate(upper, axis=2).reshape(256, 128)


def project(place, mine, other, weights):
    vmem = pl.BlockSpec(memory_space=pltpu.VMEM)
    return pl.pallas_call(
        project_kernel,
        out_shape=(
            jax.ShapeDtypeStruct((4 * mine.shape[0], WIDTH), jnp.bfloat16),
            jax.ShapeDtypeStruct((LATENT_WIDTH, 2 * VALUE_DIMS), jnp.bfloat16),
        ),
        in_specs=[pl.BlockSpec(memory_space=pltpu.SMEM)] + [vmem] * 3,
        out_specs=(vmem, vmem),
        compiler_params=pltpu.CompilerParams(vmem_limit_bytes=16 * 1024 * 1024),
        cost_estimate=pl.CostEstimate(flops=PROJECT_COST, bytes_accessed=0, transcendentals=0),
    )(place, mine, other, weights)


def attention_kernel(q_ref, vu_ref, low_ref, high_ref, bounds_ref, *refs):
    pieces, (o_ref, keys_ref, s_ref, sems) = refs[:-4], refs[-4:]
    step, many = pieces[0].shape[0], len(pieces) // 2
    fetches = []
    for i, piece in enumerate(pieces):
        fetches.append(pltpu.make_async_copy(piece, keys_ref.at[pl.ds(i * step, step), :], sems.at[i]))
        fetches[-1].start()
    q = q_ref[...]
    rows = q.shape[0]
    groups = rows // TILE
    half = groups // 2
    peaks = [jnp.full((TILE, 1), FLOOR, jnp.float32) for _ in range(groups)]
    totals = [jnp.zeros((TILE, 1), jnp.float32) for _ in range(groups)]
    summed = None
    for turn in range(2):
        for fetch in fetches[turn * many : (turn + 1) * many]:
            fetch.wait()
        highest = [jnp.full((TILE, 128), FLOOR, jnp.float32) for _ in range(groups)]
        for i in range(many):
            at = pl.ds((turn * many + i) * step, step)
            scores = lax.dot_general(
                q, keys_ref[at, :], (((1,), (1,)), ((), ())), preferred_element_type=jnp.float32
            )
            for tile in range(half):
                last = bounds_ref[pl.ds(tile * TILE, TILE), 0:1]
                first = bounds_ref[pl.ds(tile * TILE, TILE), 1:2]
                allowed = (low_ref[tile : tile + 1, at] <= last) & (high_ref[tile : tile + 1, at] >= first)
                for head in range(2):
                    g = head * half + tile
                    part = jnp.where(allowed, scores[g * TILE : (g + 1) * TILE, :], NEG)
                    s_ref[pl.ds(g * TILE, TILE), pl.ds(i * step, step)] = part
                    for lane in range(0, step, 128):
                        highest[g] = jnp.maximum(highest[g], part[:, lane : lane + 128])
        old = peaks
        peaks = [jnp.maximum(p, jnp.max(h, axis=1, keepdims=True)) for p, h in zip(old, highest)]
        sums = [jnp.zeros((TILE, 128), jnp.float32) for _ in range(groups)]
        accum = jnp.zeros((rows, LATENT_WIDTH), jnp.float32)
        for i in range(many):
            parts = []
            for g in range(groups):
                weights = jnp.exp2((s_ref[pl.ds(g * TILE, TILE), pl.ds(i * step, step)] - peaks[g]) * FACTOR)
                for lane in range(0, step, 128):
                    sums[g] = sums[g] + weights[:, lane : lane + 128]
                parts.append(weights.astype(jnp.bfloat16))
            accum = accum + jnp.dot(
                jnp.concatenate(parts, axis=0),
                keys_ref[pl.ds((turn * many + i) * step, step), 0:LATENT_WIDTH],
                preferred_element_type=jnp.float32,
            )
        sums = [jnp.sum(total, axis=1, keepdims=True) for total in sums]
        if summed is None:
            totals, summed = sums, accum
        else:
            carry = [jnp.exp2((p - new) * FACTOR) for p, new in zip(old, peaks)]
            totals = [new + total * c for new, total, c in zip(sums, totals, carry)]
            summed = accum + summed * jnp.concatenate(carry, axis=0)
    latent_out = (summed * (1.0 / jnp.concatenate(totals, axis=0))).astype(jnp.bfloat16)
    for head in range(2):
        cols = pl.ds(head * VALUE_DIMS, VALUE_DIMS)
        o_ref[:, cols] = jnp.dot(
            latent_out[head * (rows // 2) : (head + 1) * (rows // 2), :],
            vu_ref[:, cols],
            preferred_element_type=jnp.float32,
        ).astype(jnp.bfloat16)


def attention(query, value_up, pieces, low, high, bounds):
    tokens, count = query.shape[0] // 2, low.shape[1]
    vmem, hbm = pl.BlockSpec(memory_space=pltpu.VMEM), pl.BlockSpec(memory_space=pltpu.HBM)
    return pl.pallas_call(
        attention_kernel,
        out_shape=jax.ShapeDtypeStruct((tokens, 2 * VALUE_DIMS), jnp.bfloat16),
        in_specs=[vmem] * 5 + [hbm] * len(pieces),
        out_specs=vmem,
        scratch_shapes=[
            pltpu.VMEM((count, WIDTH), jnp.bfloat16),
            pltpu.VMEM((2 * tokens, count // 2), jnp.float32),
            pltpu.SemaphoreType.DMA((len(pieces),)),
        ],
        compiler_params=pltpu.CompilerParams(vmem_limit_bytes=40 * 1024 * 1024),
        cost_estimate=pl.CostEstimate(
            flops=4 * tokens * count * (576 + 512),
            bytes_accessed=count * WIDTH * 2,
            transcendentals=2 * tokens * count,
        ),
    )(query, value_up, low, high, bounds, *pieces)


def body(
    q_latent,
    kv_raw,
    query_plain_weight,
    query_rotary_weight,
    key_up_weight,
    value_up_weight,
    doc_starts,
    tile_kind,
):
    xl, z2, z1 = lax.axis_index("xl"), lax.axis_index("z2"), lax.axis_index("z1")
    y1, xh, core = lax.axis_index("y1"), lax.axis_index("xh"), lax.axis_index("c")

    kv, packed = prepare(kv_raw, query_plain_weight, query_rotary_weight, key_up_weight, value_up_weight)

    kv, packed = lax.optimization_barrier((kv, packed))
    w_pair = jnp.stack([packed, swap(packed, "xl")], axis=0)
    _, q_latent = lax.optimization_barrier((w_pair, q_latent))
    q_pair = in_order(xh, q_latent[None], swap(q_latent, "xh")[None], 0)

    near = lax.all_to_all(kv, (*Z, "y2"), 0, 0).reshape(256, WIDTH)
    weights = lax.all_gather(w_pair, Z)

    q_pair, _ = lax.optimization_barrier((q_pair, near))
    q_half = gather_direct(q_pair, ("y2", "y1"), 8)
    q_core = swap(q_half, "c")

    next_y = swap(near, "y1")
    x2_near = swap(near, "xh")
    pair = jnp.concatenate([near, next_y], axis=0)
    x1_pair = swap(pair, "xl")
    x3_pair = lax.ppermute(pair, ("xl", "xh"), [(0, 3), (3, 0), (1, 2), (2, 1)])
    x2_far, pair = lax.optimization_barrier((x2_near, pair))
    x2_next = swap(x2_far, "y1")
    x2_pair = jnp.concatenate([x2_near, x2_next], axis=0)

    query, value_up = project(jnp.stack([core, xl]), q_half.reshape(128, 1536), q_core.reshape(128, 1536), weights)

    mine = [pair, x1_pair, x2_pair, x3_pair]
    theirs = [swap(piece, "c") for piece in mine]

    shape = (2, 4, 2, 8, 4, 8)
    at = lambda d: lax.broadcasted_iota(jnp.int32, shape, d)
    far = at(1)
    k_xl, k_xh = xl ^ (far & 1), xh ^ (far >> 1)
    k_block = k_xl * 8 + at(3)
    k_y = 2 * at(4) + (y1 ^ at(2))
    k_pos = (k_block * 256 + ((k_y * 2 + k_xh) * 2 + (core ^ at(0))) * 8 + at(5)).reshape(1, 4096)
    k_tile = k_pos // TILE
    kinds = jnp.sum(
        jnp.where(
            lax.broadcasted_iota(jnp.int32, (1, 32, 4096), 1) == k_tile[:, None, :], tile_kind[:, :, None], 0
        ),
        axis=1,
    )
    big = jnp.int32(1 << 20)
    low = jnp.where(kinds == 2, k_pos, jnp.where(kinds == 1, -1, big))
    high = jnp.where(kinds == 2, k_pos, jnp.where(kinds == 1, big, -1))
    q_pos = (xl * 8 + 2 * z2 + z1) * 256 + lax.broadcasted_iota(jnp.int32, (256, 1), 0)
    q_first = jnp.max(jnp.where(doc_starts[None, :] <= q_pos, doc_starts[None, :], 0), axis=1, keepdims=True)
    bounds = jnp.concatenate([q_pos, q_first], axis=1)
    return attention(query, value_up, mine + theirs, low, high, bounds)


def solution(mesh):
    fine = Mesh(np.asarray(mesh.devices).reshape(SIZES), AXES)
    return jax.shard_map(
        body,
        mesh=fine,
        in_specs=(
            P(AXES, None),
            P(AXES, None),
            P(BLK, WIDE),
            P(BLK, WIDE),
            P(BLK, WIDE),
            P(BLK, WIDE),
            P(),
            P(BLK, None),
        ),
        out_specs=P(BLK, WIDE),
        check_vma=False,
    )
```
